256 devices in a mesh: row: 16 (over x, z_lo), col: 16 (over z_hi, y, core).
Axes of the slice: x: 4, y: 4, z: 8 (z_hi: 2, z_lo: 4; z = z_hi * 4 + z_lo), core: 2. Of those that a mesh axis runs over, the one named last changes fastest.
Arguments:
- panel: float32 [4, 49152, 256], P(None, 'row', 'col'), may hold values from -0.02734375 to 0.02734375
- t_factor: float32 [4, 256, 256], replicated, may hold values from -6 to 6
- eigvecs: float32 [49152, 4096], P('row', 'col'), may hold values from -2000 to 2000, as said below
Outputs:
- regrouped: float32 [49152, 4096], P('row', 'col')
The draws below stay inside these ranges and needn't reach their ends.
Inputs may be any that keep to these rules, and one draw needn't show every extreme that they name: `eigvecs`: Real-valued entries.
All inputs are finite; a program needn't handle non-finite values.
Results may differ from the reference program's by a relative error of at most 0.00014.
Values sent between devices are 32-bit elements; how exact they have to be, the bound alone decides.
A program may use at most 64 MiB of HBM per device.

```python
import math
import jax
import jax.numpy as jnp
from jax import lax

M = 4096
NB = 256
PANELS = 4
N = 49152
CB = 16
N_COL = 16


def draw_eigvecs(key, part):
    key = jax.random.fold_in(key, 7)
    first, second, third = jax.random.split(key, 3)
    base = jnp.clip(jax.random.normal(first, (N, M), jnp.float32), -6.0, 6.0)
    spread = math.log(10.0)
    rising = 1.0 + 2.0 * jnp.arange(N, dtype=jnp.float32) / (N - 1)
    row_scale = jnp.exp(jax.random.uniform(second, (N, 1), jnp.float32) * spread) * rising[:, None]
    col_scale = jnp.exp(jax.random.uniform(third, (1, M), jnp.float32) * spread)
    return base * row_scale * col_scale


def steps_of(key, extent, cuts, least, high):
    def one(position, shards_of):
        draws = jax.random.uniform(jax.random.fold_in(jax.random.fold_in(key, 6), position), (shards_of,), jnp.float32, least / len(cuts), high / len(cuts))
        return jnp.repeat(jnp.exp(draws), extent[position] // shards_of).reshape((-1,) + (1,) * (len(extent) - position - 1))

    loudness = one(*cuts[0])
    for cut in cuts[1:]:
        loudness = loudness * one(*cut)
    return loudness


def centred(rng, dims, scale, most, cuts=(), kind=jnp.bfloat16):
    values = jax.random.normal(rng, dims, jnp.float32) * scale
    if len(cuts) > 0:
        values = steps_of(rng, dims, cuts, -0.22, 0.18) * values
    return jnp.clip(values, min=-most, max=most).astype(kind)


def setup_inputs(seed: int = 0) -> dict:
    key_list = jax.random.split(jax.random.key(seed), 4)
    return {
        "panel": centred(key_list[0], (PANELS, N, NB), N ** -0.5, 0.02734375, ((1, 16), (2, 16)), jnp.float32),
        "t_factor": centred(key_list[1], (PANELS, NB, NB), 1.0, 6.0, (), jnp.float32),
        "eigvecs": draw_eigvecs(jax.random.fold_in(key_list[3], 71), 0),
    }


def reference(panel, t_factor, eigvecs):
    updated = eigvecs
    for index in range(PANELS):
        vectors = panel[index]
        proj = lax.dot_general(vectors, updated, (((0,), (0,)), ((), ())), precision=lax.Precision.HIGHEST, preferred_element_type=jnp.float32)
        coef = jnp.dot(jnp.triu(t_factor[index]), proj, precision=lax.Precision.HIGHEST, preferred_element_type=jnp.float32)
        updated = updated - jnp.dot(vectors, coef, precision=lax.Precision.HIGHEST, preferred_element_type=jnp.float32)
    norm_sq = lax.optimization_barrier(jnp.sum(updated * updated, axis=0))
    scaled = updated * lax.rsqrt(norm_sq / N + 1e-06)
    return scaled.reshape(N, N_COL, N_COL, CB).transpose(0, 2, 1, 3).reshape(N, M)
```

```python
import functools

import jax
import jax.numpy as jnp
from jax import lax
from jax.experimental import pallas as pl
from jax.experimental.pallas import tpu as pltpu
from jax.sharding import PartitionSpec as P

MESH = pl.DeviceIdType.MESH
F32 = jnp.float32
BF16 = jnp.bfloat16
NT = (((1,), (1,)), ((), ()))
NN = (((1,), (0,)), ((), ()))
CHUNK = 1024


def split(x):
    high = x.astype(BF16)
    return high, (x - high.astype(F32)).astype(BF16)


def dot3(ah, al, bh, bl, dims):
    dot = functools.partial(lax.dot_general, dimension_numbers=dims, preferred_element_type=F32)
    return dot(ah, bh) + dot(ah, bl) + dot(al, bh)


def kernel(
    total_rows, v_hbm, t_hbm, z_hbm, o_ref,
    zin, tin, vg, vh, vl, u, uh, ul, acc, gram, pt, px, rx, rz, ct, out, nsrc, nrecv, scl, sclr,
    loc, z_s, z_r, y_s, y_r, k_s, k_r, r_s, r_r, a_s, a_r, n_s, n_r, s_s, s_r,
):
    panels, nb, lanes = vg.shape
    row, col = lax.axis_index("row"), lax.axis_index("col")
    xi, zi = row // 4, row % 4
    hi, yi, ki = col // 8, (col // 2) % 4, col % 2

    def chip(h, y, k):
        return (row, h * 8 + y * 2 + k)

    z_peer = chip(1 - hi, yi, ki)
    k_peer = chip(hi, yi, 1 - ki)
    right, left, far = (yi + 1) % 4, (yi + 3) % 4, (yi + 2) % 4
    y_right, y_left = chip(hi, right, ki), chip(hi, left, ki)

    def at(p, h, y, start=0, size=16):
        return vg.at[p, pl.ds(pl.multiple_of((h * 8 + y * 2 + ki) * 16 + start, 8), size)]

    def remote(src, dst, send, recv, device):
        return pltpu.make_async_remote_copy(
            src_ref=src, dst_ref=dst, send_sem=send, recv_sem=recv, device_id=device, device_id_type=MESH
        )

    def own_copy(p):
        return pltpu.make_async_copy(v_hbm.at[p], at(p, hi, yi), loc.at[p])

    def z_copy(p):
        return remote(v_hbm.at[p], at(p, hi, yi), z_s.at[p], z_r.at[p], z_peer)

    def side(s):
        return hi if s == 0 else 1 - hi

    def y_copy(p, s, kind):
        h = side(s)
        if kind == 0:
            block, device = at(p, h, yi), y_right
        elif kind == 1:
            block, device = at(p, h, yi), y_left
        elif kind == 2:
            block, device = at(p, h, left, 0, 8), y_right
        else:
            block, device = at(p, h, right, 8, 8), y_left
        i = s * 4 + kind
        return remote(block, block, y_s.at[p, i], y_r.at[p, i], device)

    def k_copy(p, s, which):
        block = at(p, side(s), (yi, left, right, far)[which])
        i = s * 4 + which
        return remote(block, block, k_s.at[p, i], k_r.at[p, i], k_peer)

    def row_peer(dx, dz):
        return (((xi + dx) % 4) * 4 + (zi + dz) % 4, col)

    def rows(ref, p, start, size):
        return ref.at[p, pl.ds(pl.multiple_of(start, 8), size)]

    def rs_x(p, i):
        return remote(rows(pt, p, ((xi + i) % 4) * 64, 64), rx.at[p, i - 1], r_s.at[p, i - 1], r_r.at[p, i - 1], row_peer(i, 0))

    def rs_z(p, i):
        return remote(rows(px, p, ((zi + i) % 4) * 16, 16), rz.at[p, i - 1], r_s.at[p, 2 + i], r_r.at[p, 2 + i], row_peer(0, i))

    def ag_z(p, i):
        block = rows(ct, p, xi * 64 + zi * 16, 16)
        return remote(block, block, r_s.at[p, 5 + i], r_r.at[p, 5 + i], row_peer(0, i))

    def ag_x(p, i):
        block = rows(ct, p, xi * 64, 64)
        return remote(block, block, r_s.at[p, 8 + i], r_r.at[p, 8 + i], row_peer(i, 0))

    def regroup(i):
        to = (col + i) % 16
        return remote(
            u.at[pl.ds(pl.multiple_of(to * 16, 16), 16)],
            out.at[pl.ds(pl.multiple_of(col * 16, 16), 16)],
            a_s.at[i], a_r.at[i], (row, to),
        )

    def norms(i):
        return remote(nsrc, nrecv.at[i], n_s.at[i], n_r.at[i], ((row + i) % 16, col))

    def scales(i):
        to = (col + i) % 16
        return remote(
            scl.at[pl.ds(pl.multiple_of(to * 16, 16), 16)],
            sclr.at[pl.ds(pl.multiple_of(col * 16, 16), 16)],
            s_s.at[i], s_r.at[i], (row, to),
        )

    z_load = pltpu.make_async_copy(z_hbm, zin, loc.at[panels])
    t_load = pltpu.make_async_copy(t_hbm, tin, loc.at[panels + 1])
    for p in range(panels):
        own_copy(p).start()
    z_load.start()
    t_load.start()
    barrier = pltpu.get_barrier_semaphore()

    def greet(i, carry):
        pl.semaphore_signal(barrier, inc=1, device_id=((row + i) % 16, col), device_id_type=MESH)
        pl.semaphore_signal(barrier, inc=1, device_id=(row, (col + i) % 16), device_id_type=MESH)
        return carry

    lax.fori_loop(1, 16, greet, 0)
    for p in range(panels):
        own_copy(p).wait()
    pl.semaphore_wait(barrier, 30)

    def stage_a(p):
        z_copy(p).start()
        y_copy(p, 0, 0).start()
        y_copy(p, 0, 1).start()
        k_copy(p, 0, 0).start()

    def stage_b(p):
        z_copy(p).wait_recv()
        y_copy(p, 1, 0).start()
        y_copy(p, 1, 1).start()
        k_copy(p, 1, 0).start()

    def stage_c(p, s):
        y_copy(p, s, 0).wait_recv()
        y_copy(p, s, 2).start()
        k_copy(p, s, 1).start()
        y_copy(p, s, 1).wait_recv()
        y_copy(p, s, 3).start()
        k_copy(p, s, 2).start()

    def stage_d(p, s):
        y_copy(p, s, 2).wait_recv()
        y_copy(p, s, 3).wait_recv()
        k_copy(p, s, 3).start()

    def stage_f(p):
        for s in range(2):
            for which in range(4):
                k_copy(p, s, which).wait_recv()

    def chunks(body):
        @pl.loop(0, lanes // CHUNK)
        def _(i):
            body(pl.ds(pl.multiple_of(i * CHUNK, CHUNK), CHUNK))

    stage_a(0)
    stage_a(1)

    z_load.wait()
    t_load.wait()

    @pl.loop(0, lanes // 512)
    def _(i):
        s = pl.ds(pl.multiple_of(i * 512, 512), 512)
        block = zin[s, :].T
        u[:, s] = block
        high, low = split(block)
        uh[:, s] = high
        ul[:, s] = low

    stage_b(0)
    stage_c(0, 0)

    upper = lax.broadcasted_iota(jnp.int32, (nb, nb), 0) <= lax.broadcasted_iota(jnp.int32, (nb, nb), 1)

    def apply(p, keep):
        ch, cl = split(ct[p])

        def body(s):
            new = u[:, s] - dot3(ch, cl, vh[p, :, s], vl[p, :, s], NN)
            u[:, s] = new
            if keep:
                high, low = split(new)
                uh[:, s] = high
                ul[:, s] = low

        chunks(body)

    @pl.loop(0, panels)
    def _(p):
        stage_d(p, 0)
        stage_c(p, 1)
        stage_d(p, 1)
        stage_f(p)

        @pl.loop(0, nb // 16)
        def _(i):
            s = pl.ds(pl.multiple_of(i * 16, 16), 16)
            high, low = split(vg[p, s, :])
            vh[p, s, :] = high
            vl[p, s, :] = low

        acc[...] = dot3(uh[...], ul[...], vh[p], vl[p], NT)

        @pl.when(p > 0)
        def _():
            gram[...] = dot3(vh[p - 1], vl[p - 1], vh[p], vl[p], NT)
            for i in range(1, 4):
                ag_x(p - 1, i).wait_recv()
            ch, cl = split(ct[p - 1])
            gh, gl = split(gram[...])
            acc[...] -= dot3(ch, cl, gh, gl, NN)

        pt[p] = acc[...]
        for i in range(1, 4):
            rs_x(p, i).start()

        @pl.when(p < panels - 2)
        def _():
            stage_a(p + 2)

        @pl.when(p < panels - 1)
        def _():
            stage_b(p + 1)

        @pl.when(p > 0)
        def _():
            apply(p - 1, True)

        for i in range(1, 4):
            rs_x(p, i).wait_recv()
        px[p] = pt[p, pl.ds(pl.multiple_of(xi * 64, 64), 64)] + (rx[p, 0] + rx[p, 1] + rx[p, 2])
        for i in range(1, 4):
            rs_z(p, i).start()
        for i in range(1, 4):
            rs_z(p, i).wait_recv()
        mine = px[p, pl.ds(pl.multiple_of(zi * 16, 16), 16)] + (rz[p, 0] + rz[p, 1] + rz[p, 2])
        mh, ml = split(mine)
        th, tl = split(jnp.where(upper, tin[p], 0.0))
        ct[p, pl.ds(pl.multiple_of(xi * 64 + zi * 16, 16), 16)] = dot3(mh, ml, th, tl, NT)
        for i in range(1, 4):
            ag_z(p, i).start()

        @pl.when(p < panels - 1)
        def _():
            stage_c(p + 1, 0)

        for i in range(1, 4):
            ag_z(p, i).wait_recv()
        for i in range(1, 4):
            ag_x(p, i).start()

    for i in range(1, 4):
        ag_x(panels - 1, i).wait_recv()
    apply(panels - 1, False)

    def each(first, body):
        def step(i, carry):
            body(i)
            return carry

        lax.fori_loop(first, 16, step, 0)

    each(1, lambda i: regroup(i).start())

    squares = jnp.zeros((nb, 128), F32)
    for i in range(lanes // 128):
        block = u[:, i * 128 : (i + 1) * 128]
        squares += block * block
    partial = jnp.broadcast_to(jnp.sum(squares.T, axis=0, keepdims=True), (8, nb))
    nsrc[...] = partial
    nrecv[0] = partial
    each(1, lambda i: norms(i).start())
    each(1, lambda i: norms(i).wait_recv())
    norm_sq = jnp.sum(nrecv[...], axis=0)
    tall = jnp.broadcast_to(norm_sq[0:1], (128, nb)).T
    scl[...] = lax.rsqrt(tall / total_rows + 1e-06)
    each(1, lambda i: scales(i).start())

    def finish(source, block, scale):
        o_ref[pl.ds(pl.multiple_of(source * 16, 16), 16), :] = block * scale[:, 0:1]

    mine_at = pl.ds(pl.multiple_of(col * 16, 16), 16)
    finish(col, u[mine_at, :], scl[mine_at, :])

    def take(i):
        source = (col + 16 - i) % 16
        scales(i).wait_recv()
        regroup(i).wait_recv()
        there = pl.ds(pl.multiple_of(source * 16, 16), 16)
        finish(source, out[there, :], sclr[there, :])

    each(1, take)

    def sent(i):
        regroup(i).wait_send()
        norms(i).wait_send()
        scales(i).wait_send()

    each(1, sent)

    @pl.loop(0, panels)
    def _(p):
        z_copy(p).wait_send()
        for s in range(2):
            for kind in range(4):
                y_copy(p, s, kind).wait_send()
                k_copy(p, s, kind).wait_send()
        for i in range(1, 4):
            rs_x(p, i).wait_send()
            rs_z(p, i).wait_send()
            ag_z(p, i).wait_send()
            ag_x(p, i).wait_send()


def local(panel, t_factor, eigvecs):
    panels, lanes, width = panel.shape
    cols = eigvecs.shape[1]
    nb = t_factor.shape[1]
    vt = jnp.transpose(panel, (0, 2, 1))
    total_rows = lanes * lax.axis_size("row")
    vmem, dma = pltpu.VMEM, pltpu.SemaphoreType.DMA
    any_spec = pl.BlockSpec(memory_space=pl.ANY)
    done = pl.pallas_call(
        functools.partial(kernel, total_rows),
        out_shape=jax.ShapeDtypeStruct((cols, lanes), F32),
        in_specs=[any_spec] * 3,
        out_specs=pl.BlockSpec(memory_space=pltpu.VMEM),
        scratch_shapes=[
            vmem((lanes, cols), F32),
            vmem((panels, nb, nb), F32),
            vmem((panels, nb, lanes), F32),
            vmem((panels, nb, lanes), BF16),
            vmem((panels, nb, lanes), BF16),
            vmem((cols, lanes), F32),
            vmem((cols, lanes), BF16),
            vmem((cols, lanes), BF16),
            vmem((cols, nb), F32),
            vmem((nb, nb), F32),
            vmem((panels, cols, nb), F32),
            vmem((panels, 64, nb), F32),
            vmem((panels, 3, 64, nb), F32),
            vmem((panels, 3, 16, nb), F32),
            vmem((panels, cols, nb), F32),
            vmem((cols, lanes), F32),
            vmem((8, cols), F32),
            vmem((16, 8, cols), F32),
            vmem((cols, 128), F32),
            vmem((cols, 128), F32),
            dma((panels + 2,)),
            dma((panels,)),
            dma((panels,)),
            dma((panels, 8)),
            dma((panels, 8)),
            dma((panels, 8)),
            dma((panels, 8)),
            dma((panels, 12)),
            dma((panels, 12)),
            dma((16,)),
            dma((16,)),
            dma((16,)),
            dma((16,)),
            dma((16,)),
            dma((16,)),
        ],
        compiler_params=pltpu.CompilerParams(
            collective_id=0, has_side_effects=True, vmem_limit_bytes=60 * 2**20
        ),
    )(vt, t_factor, eigvecs)
    return jnp.transpose(done)


def solution(mesh):
    in_specs = (P(None, "row", "col"), P(), P("row", "col"))
    return jax.shard_map(local, mesh=mesh, in_specs=in_specs, out_specs=P("row", "col"), check_vma=False)
```

```python
import functools

import jax
import jax.numpy as jnp
from jax import lax
from jax.experimental import pallas as pl
from jax.experimental.pallas import tpu as pltpu
from jax.sharding import PartitionSpec as P

MESH = pl.DeviceIdType.MESH
F32 = jnp.float32
BF16 = jnp.bfloat16
NT = (((1,), (1,)), ((), ()))
NN = (((1,), (0,)), ((), ()))
CHUNK = 1024


def split(x):
    high = x.astype(BF16)
    return high, (x - high.astype(F32)).astype(BF16)


def dot3(ah, al, bh, bl, dims):
    dot = functools.partial(lax.dot_general, dimension_numbers=dims, preferred_element_type=F32)
    return dot(ah, bh) + dot(ah, bl) + dot(al, bh)


def kernel(
    total_rows, v_hbm, t_hbm, z_hbm, o_ref,
    zin, tin, vg, vh, vl, u, uh, ul, acc, gram, pt, rx, rz, ct, out, nsrc, nrecv, scl, sclr,
    loc, z_s, z_r, y_s, y_r, k_s, k_r, r_s, r_r, a_s, a_r, n_s, n_r, s_s, s_r, o_s,
):
    panels, nb, lanes = vg.shape
    half = u.shape[0] // 2
    own = half // 4
    row, col = lax.axis_index("row"), lax.axis_index("col")
    xi, zi = row // 4, row % 4
    hi, yi, ki = col // 8, (col // 2) % 4, col % 2

    def chip(h, y, k):
        return (row, h * 8 + y * 2 + k)

    z_peer = chip(1 - hi, yi, ki)
    k_peer = chip(hi, yi, 1 - ki)
    right, left, far = (yi + 1) % 4, (yi + 3) % 4, (yi + 2) % 4
    y_right, y_left = chip(hi, right, ki), chip(hi, left, ki)

    def at(p, h, y, start=0, size=16):
        return vg.at[p, pl.ds(pl.multiple_of((h * 8 + y * 2 + ki) * 16 + start, 8), size)]

    def remote(src, dst, send, recv, device):
        return pltpu.make_async_remote_copy(
            src_ref=src, dst_ref=dst, send_sem=send, recv_sem=recv, device_id=device, device_id_type=MESH
        )

    def own_copy(p):
        return pltpu.make_async_copy(v_hbm.at[p], at(p, hi, yi), loc.at[p])

    def z_copy(p):
        return remote(v_hbm.at[p], at(p, hi, yi), z_s.at[p], z_r.at[p], z_peer)

    def side(s):
        return hi if s == 0 else 1 - hi

    def y_copy(p, s, kind):
        h = side(s)
        if kind == 0:
            block, device = at(p, h, yi), y_right
        elif kind == 1:
            block, device = at(p, h, yi), y_left
        elif kind == 2:
            block, device = at(p, h, left, 0, 8), y_right
        else:
            block, device = at(p, h, right, 8, 8), y_left
        i = s * 4 + kind
        return remote(block, block, y_s.at[p, i], y_r.at[p, i], device)

    def k_copy(p, s, which):
        block = at(p, side(s), (yi, left, right, far)[which])
        i = s * 4 + which
        return remote(block, block, k_s.at[p, i], k_r.at[p, i], k_peer)

    def row_peer(dx, dz):
        return (((xi + dx) % 4) * 4 + (zi + dz) % 4, col)

    def part(ref, p, h, x):
        return ref.at[p, pl.ds(pl.multiple_of(h * half + x * own, 8), own)]

    def rs_x(p, h, i):
        to = (xi + i) % 4
        j = h * 9 + i - 1
        return remote(part(pt, p, h, to), rx.at[p, h, i - 1], r_s.at[p, j], r_r.at[p, j], row_peer(i, 0))

    def ex_z(p, h, i):
        j = h * 9 + 2 + i
        block = rz.at[p, h, zi]
        return remote(block, block, r_s.at[p, j], r_r.at[p, j], row_peer(0, i))

    def ag_x(p, h, i):
        j = h * 9 + 5 + i
        block = part(ct, p, h, xi)
        return remote(block, block, r_s.at[p, j], r_r.at[p, j], row_peer(i, 0))

    def regroup(i):
        to = col ^ i
        return remote(
            u.at[pl.ds(pl.multiple_of(to * 16, 16), 16)],
            out.at[pl.ds(pl.multiple_of(col * 16, 16), 16)],
            a_s.at[i], a_r.at[i], (row, to),
        )

    def norms(i):
        return remote(nsrc, nrecv.at[i], n_s.at[i], n_r.at[i], ((row + i) % 16, col))

    def scales(i):
        to = col ^ i
        return remote(
            scl.at[pl.ds(pl.multiple_of(to * 16, 16), 16)],
            sclr.at[pl.ds(pl.multiple_of(col * 16, 16), 16)],
            s_s.at[i], s_r.at[i], (row, to),
        )

    z_load = pltpu.make_async_copy(z_hbm, zin, loc.at[panels])
    t_load = pltpu.make_async_copy(t_hbm, tin, loc.at[panels + 1])
    for p in range(panels):
        own_copy(p).start()
    z_load.start()
    t_load.start()
    barrier = pltpu.get_barrier_semaphore()

    def greet(i, carry):
        pl.semaphore_signal(barrier, inc=1, device_id=((row + i) % 16, col), device_id_type=MESH)
        pl.semaphore_signal(barrier, inc=1, device_id=(row, (col + i) % 16), device_id_type=MESH)
        return carry

    lax.fori_loop(1, 16, greet, 0)
    for p in range(panels):
        own_copy(p).wait()
    pl.semaphore_wait(barrier, 30)

    def stage_own(p):
        y_copy(p, 0, 0).start()
        y_copy(p, 0, 1).start()
        k_copy(p, 0, 0).start()

    def stage_peer(p):
        z_copy(p).wait_recv()
        y_copy(p, 1, 0).start()
        y_copy(p, 1, 1).start()
        k_copy(p, 1, 0).start()

    def stage_relay(p, s):
        y_copy(p, s, 0).wait_recv()
        y_copy(p, s, 2).start()
        k_copy(p, s, 1).start()
        y_copy(p, s, 1).wait_recv()
        y_copy(p, s, 3).start()
        k_copy(p, s, 2).start()

    def stage_far(p, s):
        y_copy(p, s, 2).wait_recv()
        y_copy(p, s, 3).wait_recv()
        k_copy(p, s, 3).start()

    def stage_end(p):
        for s in range(2):
            for which in range(4):
                k_copy(p, s, which).wait_recv()

    def chunks(body):
        @pl.loop(0, lanes // CHUNK)
        def _(i):
            body(pl.ds(pl.multiple_of(i * CHUNK, CHUNK), CHUNK))

    z_copy(0).start()
    stage_own(0)
    stage_own(1)

    z_load.wait()
    t_load.wait()

    @pl.loop(0, lanes // 512)
    def _(i):
        s = pl.ds(pl.multiple_of(i * 512, 512), 512)
        block = zin[s, :].T
        u[:, s] = block
        high, low = split(block)
        uh[:, s] = high
        ul[:, s] = low

    stage_relay(0, 0)
    stage_peer(0)
    z_copy(1).start()
    z_copy(2).start()
    stage_relay(1, 0)
    stage_far(0, 0)
    stage_relay(0, 1)
    stage_own(2)
    stage_peer(1)
    z_copy(3).start()
    stage_far(0, 1)
    stage_end(0)

    upper = lax.broadcasted_iota(jnp.int32, (nb, nb), 0) <= lax.broadcasted_iota(jnp.int32, (nb, nb), 1)

    def apply(p, keep):
        ch, cl = split(ct[p])

        def body(s):
            new = u[:, s] - dot3(ch, cl, vh[p, :, s], vl[p, :, s], NN)
            u[:, s] = new
            if keep:
                high, low = split(new)
                uh[:, s] = high
                ul[:, s] = low

        chunks(body)

    @pl.loop(0, panels)
    def _(p):
        @pl.loop(0, nb // 16)
        def _(i):
            s = pl.ds(pl.multiple_of(i * 16, 16), 16)
            high, low = split(vg[p, s, :])
            vh[p, s, :] = high
            vl[p, s, :] = low

        acc[...] = dot3(uh[...], ul[...], vh[p], vl[p], NT)

        @pl.when(p > 0)
        def _():
            gram[...] = dot3(vh[p - 1], vl[p - 1], vh[p], vl[p], NT)
            for h in range(2):
                for i in range(1, 4):
                    ag_x(p - 1, h, i).wait_recv()
            ch, cl = split(ct[p - 1])
            gh, gl = split(gram[...])
            acc[...] -= dot3(ch, cl, gh, gl, NN)

        pt[p] = acc[...]
        for h in range(2):
            for i in range(1, 4):
                rs_x(p, h, i).start()

        @pl.when(p < panels - 1)
        def _():
            stage_relay(p + 1, 1)

        @pl.when(p < panels - 2)
        def _():
            stage_relay(p + 2, 0)

        @pl.when(p > 0)
        def _():
            apply(p - 1, True)

        for h in range(2):
            for i in range(1, 4):
                rs_x(p, h, i).wait_recv()
            mine = pl.ds(pl.multiple_of(h * half + xi * own, 8), own)
            rz[p, h, zi] = pt[p, mine] + (rx[p, h, 0] + rx[p, h, 1] + rx[p, h, 2])
            for i in range(1, 4):
                ex_z(p, h, i).start()

        @pl.when(p < panels - 2)
        def _():
            stage_peer(p + 2)

        th, tl = split(jnp.where(upper, tin[p], 0.0))
        for h in range(2):
            for i in range(1, 4):
                ex_z(p, h, i).wait_recv()
            mh, ml = split((rz[p, h, 0] + rz[p, h, 1]) + (rz[p, h, 2] + rz[p, h, 3]))
            mine = pl.ds(pl.multiple_of(h * half + xi * own, 8), own)
            ct[p, mine] = dot3(mh, ml, th, tl, NT)
            for i in range(1, 4):
                ag_x(p, h, i).start()

        @pl.when(p < panels - 3)
        def _():
            stage_own(p + 3)

        @pl.when(p < panels - 1)
        def _():
            stage_far(p + 1, 0)
            stage_far(p + 1, 1)
            stage_end(p + 1)

    for h in range(2):
        for i in range(1, 4):
            ag_x(panels - 1, h, i).wait_recv()
    apply(panels - 1, False)

    def each(first, body):
        def step(i, carry):
            body(i)
            return carry

        lax.fori_loop(first, 16, step, 0)

    squares = jnp.zeros((nb, 128), F32)
    for i in range(lanes // 128):
        block = u[:, i * 128 : (i + 1) * 128]
        squares += block * block
    partial = jnp.broadcast_to(jnp.sum(squares.T, axis=0, keepdims=True), (8, nb))
    nsrc[...] = partial
    nrecv[0] = partial
    each(1, lambda i: norms(i).start())
    each(1, lambda i: regroup(16 - i).start())
    each(1, lambda i: norms(i).wait_recv())
    norm_sq = jnp.sum(nrecv[...], axis=0)
    tall = jnp.broadcast_to(norm_sq[0:1], (128, nb)).T
    scl[...] = lax.rsqrt(tall / total_rows + 1e-06)
    each(1, lambda i: scales(i).start())

    def there(source):
        return pl.ds(pl.multiple_of(source * 16, 16), 16)

    def store(source):
        return pltpu.make_async_copy(out.at[there(source)], o_ref.at[there(source)], o_s.at[source])

    out[there(col), :] = u[there(col), :] * scl[there(col), 0:1]
    store(col).start()

    def take(i):
        source = col ^ i
        scales(i).wait_recv()
        regroup(i).wait_recv()
        out[there(source), :] = out[there(source), :] * sclr[there(source), 0:1]
        store(source).start()

    each(1, take)
    store(col).wait()
    each(1, lambda i: store(col ^ i).wait())

    def sent(i):
        regroup(i).wait_send()
        norms(i).wait_send()
        scales(i).wait_send()

    each(1, sent)

    @pl.loop(0, panels)
    def _(p):
        z_copy(p).wait_send()
        for s in range(2):
            for kind in range(4):
                y_copy(p, s, kind).wait_send()
                k_copy(p, s, kind).wait_send()
        for h in range(2):
            for i in range(1, 4):
                rs_x(p, h, i).wait_send()
                ex_z(p, h, i).wait_send()
                ag_x(p, h, i).wait_send()


def local(panel, t_factor, eigvecs):
    panels, lanes, width = panel.shape
    cols = eigvecs.shape[1]
    nb = t_factor.shape[1]
    vt = jnp.transpose(panel, (0, 2, 1))
    total_rows = lanes * lax.axis_size("row")
    vmem, dma = pltpu.VMEM, pltpu.SemaphoreType.DMA
    any_spec = pl.BlockSpec(memory_space=pl.ANY)
    done = pl.pallas_call(
        functools.partial(kernel, total_rows),
        out_shape=jax.ShapeDtypeStruct((cols, lanes), F32),
        in_specs=[any_spec] * 3,
        out_specs=any_spec,
        scratch_shapes=[
            vmem((lanes, cols), F32),
            vmem((panels, nb, nb), F32),
            vmem((panels, nb, lanes), F32),
            vmem((panels, nb, lanes), BF16),
            vmem((panels, nb, lanes), BF16),
            vmem((cols, lanes), F32),
            vmem((cols, lanes), BF16),
            vmem((cols, lanes), BF16),
            vmem((cols, nb), F32),
            vmem((nb, nb), F32),
            vmem((panels, cols, nb), F32),
            vmem((panels, 2, 3, cols // 8, nb), F32),
            vmem((panels, 2, 4, cols // 8, nb), F32),
            vmem((panels, cols, nb), F32),
            vmem((cols, lanes), F32),
            vmem((8, cols), F32),
            vmem((16, 8, cols), F32),
            vmem((cols, 128), F32),
            vmem((cols, 128), F32),
            dma((panels + 2,)),
            dma((panels,)),
            dma((panels,)),
            dma((panels, 8)),
            dma((panels, 8)),
            dma((panels, 8)),
            dma((panels, 8)),
            dma((panels, 18)),
            dma((panels, 18)),
            dma((16,)),
            dma((16,)),
            dma((16,)),
            dma((16,)),
            dma((16,)),
            dma((16,)),
            dma((16,)),
        ],
        compiler_params=pltpu.CompilerParams(
            collective_id=0, has_side_effects=True, vmem_limit_bytes=60 * 2**20
        ),
    )(vt, t_factor, eigvecs)
    return jnp.transpose(done)


def solution(mesh):
    in_specs = (P(None, "row", "col"), P(), P("row", "col"))
    return jax.shard_map(local, mesh=mesh, in_specs=in_specs, out_specs=P("row", "col"), check_vma=False)
```

```python
import functools

import jax
import jax.numpy as jnp
from jax import lax
from jax.experimental import pallas as pl
from jax.experimental.pallas import tpu as pltpu
from jax.sharding import PartitionSpec as P

MESH = pl.DeviceIdType.MESH
F32 = jnp.float32
BF16 = jnp.bfloat16
NT = (((1,), (1,)), ((), ()))
NN = (((1,), (0,)), ((), ()))
CHUNK = 1024


def split(x):
    high = x.astype(BF16)
    return high, (x - high.astype(F32)).astype(BF16)


def dot3(ah, al, bh, bl, dims):
    dot = functools.partial(lax.dot_general, dimension_numbers=dims, preferred_element_type=F32)
    return dot(ah, bh) + dot(ah, bl) + dot(al, bh)


def kernel(
    total_rows, v_hbm, t_hbm, z_hbm, o_ref,
    zin, tin, vg, vh, vl, u, uh, ul, acc, gram, pt, rx, rz, ct, early, ua, ca, out, nsrc, nrecv, scl, sclr,
    loc, z_s, z_r, y_s, y_r, k_s, k_r, r_s, r_r, a_s, a_r, n_s, n_r, s_s, s_r, o_s, e_s, e_r, c_s, c_r,
):
    panels, nb, lanes = vg.shape
    half = u.shape[0] // 2
    own = half // 4
    row, col = lax.axis_index("row"), lax.axis_index("col")
    xi, zi = row // 4, row % 4
    hi, yi, ki = col // 8, (col // 2) % 4, col % 2
    ci = col % 8

    def chip(h, y, k):
        return (row, h * 8 + y * 2 + k)

    z_peer = chip(1 - hi, yi, ki)
    k_peer = chip(hi, yi, 1 - ki)
    right, left, far = (yi + 1) % 4, (yi + 3) % 4, (yi + 2) % 4
    y_right, y_left = chip(hi, right, ki), chip(hi, left, ki)

    def at(p, h, y, start=0, size=16):
        return vg.at[p, pl.ds(pl.multiple_of((h * 8 + y * 2 + ki) * 16 + start, 8), size)]

    def remote(src, dst, send, recv, device):
        return pltpu.make_async_remote_copy(
            src_ref=src, dst_ref=dst, send_sem=send, recv_sem=recv, device_id=device, device_id_type=MESH
        )

    def own_copy(p):
        return pltpu.make_async_copy(v_hbm.at[p], at(p, hi, yi), loc.at[p])

    def z_copy(p):
        return remote(v_hbm.at[p], at(p, hi, yi), z_s.at[p], z_r.at[p], z_peer)

    def side(s):
        return hi if s == 0 else 1 - hi

    def y_copy(p, s, kind):
        h = side(s)
        if kind == 0:
            block, device = at(p, h, yi), y_right
        elif kind == 1:
            block, device = at(p, h, yi), y_left
        elif kind == 2:
            block, device = at(p, h, left, 0, 8), y_right
        else:
            block, device = at(p, h, right, 8, 8), y_left
        i = s * 4 + kind
        return remote(block, block, y_s.at[p, i], y_r.at[p, i], device)

    def k_copy(p, s, which):
        block = at(p, side(s), (yi, left, right, far)[which])
        i = s * 4 + which
        return remote(block, block, k_s.at[p, i], k_r.at[p, i], k_peer)

    def row_peer(dx, dz):
        return (((xi + dx) % 4) * 4 + (zi + dz) % 4, col)

    def part(ref, p, h, x):
        return ref.at[p, pl.ds(pl.multiple_of(h * half + x * own, 8), own)]

    def rs_x(p, h, i):
        to = (xi + i) % 4
        j = h * 9 + i - 1
        return remote(part(pt, p, h, to), rx.at[p, h, i - 1], r_s.at[p, j], r_r.at[p, j], row_peer(i, 0))

    def ex_z(p, h, i):
        j = h * 9 + 2 + i
        block = rz.at[p, h, zi]
        return remote(block, block, r_s.at[p, j], r_r.at[p, j], row_peer(0, i))

    def ag_x(p, h, i):
        j = h * 9 + 5 + i
        block = part(ct, p, h, xi)
        return remote(block, block, r_s.at[p, j], r_r.at[p, j], row_peer(i, 0))

    def eight(i):
        return pl.ds(pl.multiple_of(i * 8, 8), 8)

    def sixteen(i):
        return pl.ds(pl.multiple_of(i * 16, 16), 16)

    def across(i):
        return (1 - hi) * 8 + (ci ^ i)

    def move_soon(i):
        return remote(early.at[eight(ci ^ i)], ua.at[eight(ci)], e_s.at[i], e_r.at[i], (row, across(i)))

    def coef(p, i):
        return remote(ct.at[p, eight(across(i) * 2)], ca.at[p, eight(ci)], c_s.at[p, i], c_r.at[p, i], (row, across(i)))

    def move_across(i):
        return remote(u.at[eight(across(i) * 2 + 1)], out.at[eight(col * 2 + 1)], a_s.at[8 + i], a_r.at[8 + i], (row, across(i)))

    def move_beside(i):
        to = col ^ i
        return remote(u.at[sixteen(to)], out.at[sixteen(col)], a_s.at[i], a_r.at[i], (row, to))

    def norms(i):
        return remote(nsrc, nrecv.at[i], n_s.at[i], n_r.at[i], ((row + i) % 16, col))

    def scales(i):
        to = col ^ i
        return remote(
            scl.at[pl.ds(pl.multiple_of(to * 16, 16), 16)],
            sclr.at[pl.ds(pl.multiple_of(col * 16, 16), 16)],
            s_s.at[i], s_r.at[i], (row, to),
        )

    z_load = pltpu.make_async_copy(z_hbm, zin, loc.at[panels])
    t_load = pltpu.make_async_copy(t_hbm, tin, loc.at[panels + 1])
    for p in range(panels):
        own_copy(p).start()
    z_load.start()
    t_load.start()
    barrier = pltpu.get_barrier_semaphore()

    def greet(i, carry):
        pl.semaphore_signal(barrier, inc=1, device_id=((row + i) % 16, col), device_id_type=MESH)
        pl.semaphore_signal(barrier, inc=1, device_id=(row, (col + i) % 16), device_id_type=MESH)
        return carry

    lax.fori_loop(1, 16, greet, 0)
    for p in range(panels):
        own_copy(p).wait()
    pl.semaphore_wait(barrier, 30)

    def stage_own(p):
        y_copy(p, 0, 0).start()
        y_copy(p, 0, 1).start()
        k_copy(p, 0, 0).start()

    def stage_peer(p):
        z_copy(p).wait_recv()
        y_copy(p, 1, 0).start()
        y_copy(p, 1, 1).start()
        k_copy(p, 1, 0).start()

    def stage_relay(p, s):
        y_copy(p, s, 0).wait_recv()
        y_copy(p, s, 2).start()
        k_copy(p, s, 1).start()
        y_copy(p, s, 1).wait_recv()
        y_copy(p, s, 3).start()
        k_copy(p, s, 2).start()

    def stage_far(p, s):
        y_copy(p, s, 2).wait_recv()
        y_copy(p, s, 3).wait_recv()
        k_copy(p, s, 3).start()

    def stage_end(p):
        for s in range(2):
            for which in range(4):
                k_copy(p, s, which).wait_recv()

    def chunks(body):
        @pl.loop(0, lanes // CHUNK)
        def _(i):
            body(pl.ds(pl.multiple_of(i * CHUNK, CHUNK), CHUNK))

    z_copy(0).start()
    stage_own(0)
    stage_own(1)

    z_load.wait()
    t_load.wait()

    @pl.loop(0, lanes // 512)
    def _(i):
        s = pl.ds(pl.multiple_of(i * 512, 512), 512)
        block = zin[s, :].T
        u[:, s] = block
        high, low = split(block)
        uh[:, s] = high
        ul[:, s] = low
        crossing = zin[s, pl.ds(pl.multiple_of((1 - hi) * 128, 128), 128)].T.reshape(8, 16, 512)
        early[:, s] = crossing[:, 0:8].reshape(64, 512)

    stage_relay(0, 0)
    stage_peer(0)
    z_copy(1).start()
    z_copy(2).start()
    stage_relay(1, 0)
    stage_far(0, 0)
    stage_relay(0, 1)
    stage_own(2)
    stage_peer(1)
    z_copy(3).start()
    stage_far(0, 1)
    stage_end(0)

    def each(first, last, body):
        def step(i, carry):
            body(i)
            return carry

        lax.fori_loop(first, last, step, 0)

    upper = lax.broadcasted_iota(jnp.int32, (nb, nb), 0) <= lax.broadcasted_iota(jnp.int32, (nb, nb), 1)

    def apply(p, keep):
        ch, cl = split(ct[p])

        def body(s):
            new = u[:, s] - dot3(ch, cl, vh[p, :, s], vl[p, :, s], NN)
            u[:, s] = new
            if keep:
                high, low = split(new)
                uh[:, s] = high
                ul[:, s] = low

        chunks(body)

    @pl.loop(0, panels)
    def _(p):
        @pl.loop(0, nb // 16)
        def _(i):
            s = pl.ds(pl.multiple_of(i * 16, 16), 16)
            high, low = split(vg[p, s, :])
            vh[p, s, :] = high
            vl[p, s, :] = low

        acc[...] = dot3(uh[...], ul[...], vh[p], vl[p], NT)

        @pl.when(p > 0)
        def _():
            gram[...] = dot3(vh[p - 1], vl[p - 1], vh[p], vl[p], NT)
            for h in range(2):
                for i in range(1, 4):
                    ag_x(p - 1, h, i).wait_recv()
            each(0, 8, lambda i: coef(p - 1, i).start())
            ch, cl = split(ct[p - 1])
            gh, gl = split(gram[...])
            acc[...] -= dot3(ch, cl, gh, gl, NN)

        pt[p] = acc[...]
        for h in range(2):
            for i in range(1, 4):
                rs_x(p, h, i).start()

        @pl.when(p < panels - 1)
        def _():
            stage_relay(p + 1, 1)

        @pl.when(p < panels - 2)
        def _():
            stage_relay(p + 2, 0)

        @pl.when(p > 0)
        def _():
            apply(p - 1, True)

        for h in range(2):
            for i in range(1, 4):
                rs_x(p, h, i).wait_recv()
            mine = pl.ds(pl.multiple_of(h * half + xi * own, 8), own)
            rz[p, h, zi] = pt[p, mine] + (rx[p, h, 0] + rx[p, h, 1] + rx[p, h, 2])
            for i in range(1, 4):
                ex_z(p, h, i).start()

        @pl.when(p < panels - 2)
        def _():
            stage_peer(p + 2)

        th, tl = split(jnp.where(upper, tin[p], 0.0))
        for h in range(2):
            for i in range(1, 4):
                ex_z(p, h, i).wait_recv()
            mh, ml = split((rz[p, h, 0] + rz[p, h, 1]) + (rz[p, h, 2] + rz[p, h, 3]))
            mine = pl.ds(pl.multiple_of(h * half + xi * own, 8), own)
            ct[p, mine] = dot3(mh, ml, th, tl, NT)
            for i in range(1, 4):
                ag_x(p, h, i).start()

        each(p * 2, p * 2 + 2, lambda i: move_soon(i).start())

        @pl.when(p < panels - 3)
        def _():
            stage_own(p + 3)

        @pl.when(p < panels - 1)
        def _():
            stage_far(p + 1, 0)
            stage_far(p + 1, 1)
            stage_end(p + 1)

    for h in range(2):
        for i in range(1, 4):
            ag_x(panels - 1, h, i).wait_recv()
    each(0, 8, lambda i: coef(panels - 1, i).start())
    apply(panels - 1, False)

    squares = jnp.zeros((nb, 128), F32)
    for i in range(lanes // 128):
        block = u[:, i * 128 : (i + 1) * 128]
        squares += block * block
    partial = jnp.broadcast_to(jnp.sum(squares.T, axis=0, keepdims=True), (8, nb))
    nsrc[...] = partial
    nrecv[0] = partial
    each(1, 16, lambda i: norms(i).start())
    each(1, 8, lambda i: move_beside(i).start())
    each(1, 16, lambda i: norms(i).wait_recv())
    norm_sq = jnp.sum(nrecv[...], axis=0)
    tall = jnp.broadcast_to(norm_sq[0:1], (128, nb)).T
    scl[...] = lax.rsqrt(tall / total_rows + 1e-06)
    each(1, 16, lambda i: scales(i).start())
    each(0, 8, lambda i: move_across(i).start())

    each(0, 8, lambda i: move_soon(i).wait_recv())

    @pl.loop(0, panels)
    def _(p):
        each(0, 8, lambda i: coef(p, i).wait_recv())
        ch, cl = split(ca[p])

        def body(s):
            ua[:, s] -= dot3(ch, cl, vh[p, :, s], vl[p, :, s], NN)

        chunks(body)

    def store(source):
        return pltpu.make_async_copy(out.at[sixteen(source)], o_ref.at[sixteen(source)], o_s.at[source])

    out[sixteen(col), :] = u[sixteen(col), :] * scl[sixteen(col), 0:1]
    store(col).start()

    def take_beside(i):
        source = col ^ i
        scales(i).wait_recv()
        move_beside(i).wait_recv()
        out[sixteen(source), :] = out[sixteen(source), :] * sclr[sixteen(source), 0:1]
        store(source).start()

    each(1, 8, take_beside)

    def take_across(i):
        source = across(i)
        scales(8 + i).wait_recv()
        low, high = eight(source * 2), eight(source * 2 + 1)
        out[low, :] = ua[eight(ci ^ i), :] * sclr[low, 0:1]
        move_across(i).wait_recv()
        out[high, :] = out[high, :] * sclr[high, 0:1]
        store(source).start()

    each(0, 8, take_across)
    each(0, 16, lambda i: store(i).wait())

    def sent(i):
        norms(i).wait_send()
        scales(i).wait_send()

    each(1, 16, sent)
    each(1, 8, lambda i: move_beside(i).wait_send())

    def sent_across(i):
        move_soon(i).wait_send()
        move_across(i).wait_send()

    each(0, 8, sent_across)

    @pl.loop(0, panels)
    def _(p):
        z_copy(p).wait_send()
        each(0, 8, lambda i: coef(p, i).wait_send())
        for s in range(2):
            for kind in range(4):
                y_copy(p, s, kind).wait_send()
                k_copy(p, s, kind).wait_send()
        for h in range(2):
            for i in range(1, 4):
                rs_x(p, h, i).wait_send()
                ex_z(p, h, i).wait_send()
                ag_x(p, h, i).wait_send()


def local(panel, t_factor, eigvecs):
    panels, lanes, width = panel.shape
    cols = eigvecs.shape[1]
    nb = t_factor.shape[1]
    vt = jnp.transpose(panel, (0, 2, 1))
    total_rows = lanes * lax.axis_size("row")
    vmem, dma = pltpu.VMEM, pltpu.SemaphoreType.DMA
    any_spec = pl.BlockSpec(memory_space=pl.ANY)
    done = pl.pallas_call(
        functools.partial(kernel, total_rows),
        out_shape=jax.ShapeDtypeStruct((cols, lanes), F32),
        in_specs=[any_spec] * 3,
        out_specs=any_spec,
        scratch_shapes=[
            vmem((lanes, cols), F32),
            vmem((panels, nb, nb), F32),
            vmem((panels, nb, lanes), F32),
            vmem((panels, nb, lanes), BF16),
            vmem((panels, nb, lanes), BF16),
            vmem((cols, lanes), F32),
            vmem((cols, lanes), BF16),
            vmem((cols, lanes), BF16),
            vmem((cols, nb), F32),
            vmem((nb, nb), F32),
            vmem((panels, cols, nb), F32),
            vmem((panels, 2, 3, cols // 8, nb), F32),
            vmem((panels, 2, 4, cols // 8, nb), F32),
            vmem((panels, cols, nb), F32),
            vmem((cols // 4, lanes), F32),
            vmem((cols // 4, lanes), F32),
            vmem((panels, cols // 4, nb), F32),
            vmem((cols, lanes), F32),
            vmem((8, cols), F32),
            vmem((16, 8, cols), F32),
            vmem((cols, 128), F32),
            vmem((cols, 128), F32),
            dma((panels + 2,)),
            dma((panels,)),
            dma((panels,)),
            dma((panels, 8)),
            dma((panels, 8)),
            dma((panels, 8)),
            dma((panels, 8)),
            dma((panels, 18)),
            dma((panels, 18)),
            dma((16,)),
            dma((16,)),
            dma((16,)),
            dma((16,)),
            dma((16,)),
            dma((16,)),
            dma((16,)),
            dma((8,)),
            dma((8,)),
            dma((panels, 8)),
            dma((panels, 8)),
        ],
        compiler_params=pltpu.CompilerParams(
            collective_id=0, has_side_effects=True, vmem_limit_bytes=60 * 2**20
        ),
    )(vt, t_factor, eigvecs)
    return jnp.transpose(done)


def solution(mesh):
    in_specs = (P(None, "row", "col"), P(), P("row", "col"))
    return jax.shard_map(local, mesh=mesh, in_specs=in_specs, out_specs=P("row", "col"), check_vma=False)
```

```python
import functools

import jax
import jax.numpy as jnp
from jax import lax
from jax.experimental import pallas as pl
from jax.experimental.pallas import tpu as pltpu
from jax.sharding import PartitionSpec as P

MESH = pl.DeviceIdType.MESH
F32 = jnp.float32
BF16 = jnp.bfloat16
NT = (((1,), (1,)), ((), ()))
NN = (((1,), (0,)), ((), ()))
CHUNK = 1024


def split(x):
    high = x.astype(BF16)
    return high, (x - high.astype(F32)).astype(BF16)


def dot3(ah, al, bh, bl, dims):
    dot = functools.partial(lax.dot_general, dimension_numbers=dims, preferred_element_type=F32)
    return dot(ah, bh) + dot(ah, bl) + dot(al, bh)


def kernel(
    total_rows, v_hbm, t_hbm, z_hbm, o_ref,
    zin, tin, vg, vh, vl, u, uh, ul, acc, gram, pt, rx, rz, ct, early, ua, ca, out, nsrc, nrecv, scl, sclr,
    loc, z_s, z_r, y_s, y_r, k_s, k_r, r_s, r_r, a_s, a_r, n_s, n_r, s_s, s_r, o_s, e_s, e_r, c_s, c_r,
):
    panels, nb, lanes = vg.shape
    half = u.shape[0] // 2
    own = half // 4
    row, col = lax.axis_index("row"), lax.axis_index("col")
    xi, zi = row // 4, row % 4
    hi, yi, ki = col // 8, (col // 2) % 4, col % 2
    ci = col % 8

    def chip(h, y, k):
        return (row, h * 8 + y * 2 + k)

    z_peer = chip(1 - hi, yi, ki)
    k_peer = chip(hi, yi, 1 - ki)
    right, left, far = (yi + 1) % 4, (yi + 3) % 4, (yi + 2) % 4
    y_right, y_left = chip(hi, right, ki), chip(hi, left, ki)

    def at(p, h, y, start=0, size=16):
        return vg.at[p, pl.ds(pl.multiple_of((h * 8 + y * 2 + ki) * 16 + start, 8), size)]

    def remote(src, dst, send, recv, device):
        return pltpu.make_async_remote_copy(
            src_ref=src, dst_ref=dst, send_sem=send, recv_sem=recv, device_id=device, device_id_type=MESH
        )

    def own_copy(p):
        return pltpu.make_async_copy(v_hbm.at[p], at(p, hi, yi), loc.at[p])

    def z_copy(p):
        return remote(v_hbm.at[p], at(p, hi, yi), z_s.at[p], z_r.at[p], z_peer)

    def side(s):
        return hi if s == 0 else 1 - hi

    def y_copy(p, s, kind):
        h = side(s)
        if kind == 0:
            block, device = at(p, h, yi), y_right
        elif kind == 1:
            block, device = at(p, h, yi), y_left
        elif kind == 2:
            block, device = at(p, h, left, 0, 8), y_right
        else:
            block, device = at(p, h, right, 8, 8), y_left
        i = s * 4 + kind
        return remote(block, block, y_s.at[p, i], y_r.at[p, i], device)

    def k_copy(p, s, which):
        block = at(p, side(s), (yi, left, right, far)[which])
        i = s * 4 + which
        return remote(block, block, k_s.at[p, i], k_r.at[p, i], k_peer)

    def row_peer(dx, dz):
        return (((xi + dx) % 4) * 4 + (zi + dz) % 4, col)

    def part(ref, p, h, x):
        return ref.at[p, pl.ds(pl.multiple_of(h * half + x * own, 8), own)]

    def rs_x(p, h, i):
        to = (xi + i) % 4
        j = h * 9 + i - 1
        return remote(part(pt, p, h, to), rx.at[p, h, i - 1], r_s.at[p, j], r_r.at[p, j], row_peer(i, 0))

    def ex_z(p, h, i):
        j = h * 9 + 2 + i
        block = rz.at[p, h, zi]
        return remote(block, block, r_s.at[p, j], r_r.at[p, j], row_peer(0, i))

    def ag_x(p, h, i):
        j = h * 9 + 5 + i
        block = part(ct, p, h, xi)
        return remote(block, block, r_s.at[p, j], r_r.at[p, j], row_peer(i, 0))

    def eight(i):
        return pl.ds(pl.multiple_of(i * 8, 8), 8)

    def sixteen(i):
        return pl.ds(pl.multiple_of(i * 16, 16), 16)

    def across(i):
        return (1 - hi) * 8 + (ci ^ i)

    def move_soon(i):
        return remote(early.at[eight(ci ^ i)], ua.at[eight(ci)], e_s.at[i], e_r.at[i], (row, across(i)))

    def coef(p, i):
        return remote(ct.at[p, eight(across(i) * 2)], ca.at[p, eight(ci)], c_s.at[p, i], c_r.at[p, i], (row, across(i)))

    def move_across(i):
        return remote(u.at[eight(across(i) * 2 + 1)], out.at[eight(col * 2 + 1)], a_s.at[8 + i], a_r.at[8 + i], (row, across(i)))

    def move_beside(i):
        to = col ^ i
        return remote(u.at[sixteen(to)], out.at[sixteen(col)], a_s.at[i], a_r.at[i], (row, to))

    def norms(i):
        return remote(nsrc, nrecv.at[i], n_s.at[i], n_r.at[i], ((row + i) % 16, col))

    def scales(i):
        to = col ^ i
        return remote(
            scl.at[pl.ds(pl.multiple_of(to * 16, 16), 16)],
            sclr.at[pl.ds(pl.multiple_of(col * 16, 16), 16)],
            s_s.at[i], s_r.at[i], (row, to),
        )

    z_load = pltpu.make_async_copy(z_hbm, zin, loc.at[panels])
    t_load = pltpu.make_async_copy(t_hbm, tin, loc.at[panels + 1])
    for p in range(panels):
        own_copy(p).start()
    z_load.start()
    t_load.start()
    barrier = pltpu.get_barrier_semaphore()

    def greet(i, carry):
        pl.semaphore_signal(barrier, inc=1, device_id=((row + i) % 16, col), device_id_type=MESH)
        pl.semaphore_signal(barrier, inc=1, device_id=(row, (col + i) % 16), device_id_type=MESH)
        return carry

    lax.fori_loop(1, 16, greet, 0)
    for p in range(panels):
        own_copy(p).wait()
    pl.semaphore_wait(barrier, 30)

    def stage_own(p):
        y_copy(p, 0, 0).start()
        y_copy(p, 0, 1).start()
        k_copy(p, 0, 0).start()

    def stage_peer(p):
        z_copy(p).wait_recv()
        y_copy(p, 1, 0).start()
        y_copy(p, 1, 1).start()
        k_copy(p, 1, 0).start()

    def stage_relay(p, s):
        y_copy(p, s, 0).wait_recv()
        y_copy(p, s, 2).start()
        k_copy(p, s, 1).start()
        y_copy(p, s, 1).wait_recv()
        y_copy(p, s, 3).start()
        k_copy(p, s, 2).start()

    def stage_far(p, s):
        y_copy(p, s, 2).wait_recv()
        y_copy(p, s, 3).wait_recv()
        k_copy(p, s, 3).start()

    def stage_end(p):
        for s in range(2):
            for which in range(4):
                k_copy(p, s, which).wait_recv()

    def chunks(body):
        @pl.loop(0, lanes // CHUNK)
        def _(i):
            body(pl.ds(pl.multiple_of(i * CHUNK, CHUNK), CHUNK))

    for p in range(panels):
        z_copy(p).start()
    stage_own(0)
    stage_own(1)

    z_load.wait()
    t_load.wait()

    @pl.loop(0, lanes // 512)
    def _(i):
        s = pl.ds(pl.multiple_of(i * 512, 512), 512)
        block = zin[s, :].T
        u[:, s] = block
        high, low = split(block)
        uh[:, s] = high
        ul[:, s] = low
        crossing = zin[s, pl.ds(pl.multiple_of((1 - hi) * 128, 128), 128)].T.reshape(8, 16, 512)
        early[:, s] = crossing[:, 0:8].reshape(64, 512)

    stage_relay(0, 0)
    stage_peer(0)
    stage_relay(1, 0)
    stage_own(2)
    stage_far(0, 0)
    stage_relay(0, 1)
    stage_peer(1)
    stage_far(0, 1)
    stage_end(0)

    def each(first, last, body):
        def step(i, carry):
            body(i)
            return carry

        lax.fori_loop(first, last, step, 0)

    upper = lax.broadcasted_iota(jnp.int32, (nb, nb), 0) <= lax.broadcasted_iota(jnp.int32, (nb, nb), 1)

    def apply(p, keep):
        ch, cl = split(ct[p])

        def body(s):
            new = u[:, s] - dot3(ch, cl, vh[p, :, s], vl[p, :, s], NN)
            u[:, s] = new
            if keep:
                high, low = split(new)
                uh[:, s] = high
                ul[:, s] = low

        chunks(body)

    @pl.loop(0, panels)
    def _(p):
        @pl.loop(0, nb // 16)
        def _(i):
            s = pl.ds(pl.multiple_of(i * 16, 16), 16)
            high, low = split(vg[p, s, :])
            vh[p, s, :] = high
            vl[p, s, :] = low

        acc[...] = dot3(uh[...], ul[...], vh[p], vl[p], NT)

        @pl.when(p > 0)
        def _():
            gram[...] = dot3(vh[p - 1], vl[p - 1], vh[p], vl[p], NT)
            for h in range(2):
                for i in range(1, 4):
                    ag_x(p - 1, h, i).wait_recv()
            each(0, 8, lambda i: coef(p - 1, i).start())
            ch, cl = split(ct[p - 1])
            gh, gl = split(gram[...])
            acc[...] -= dot3(ch, cl, gh, gl, NN)

        pt[p] = acc[...]
        for h in range(2):
            for i in range(1, 4):
                rs_x(p, h, i).start()

        @pl.when(p < panels - 1)
        def _():
            stage_relay(p + 1, 1)

        @pl.when(p > 0)
        def _():
            apply(p - 1, True)

        for h in range(2):
            for i in range(1, 4):
                rs_x(p, h, i).wait_recv()
            mine = pl.ds(pl.multiple_of(h * half + xi * own, 8), own)
            rz[p, h, zi] = pt[p, mine] + (rx[p, h, 0] + rx[p, h, 1] + rx[p, h, 2])
            for i in range(1, 4):
                ex_z(p, h, i).start()

        @pl.when(p < panels - 2)
        def _():
            stage_relay(p + 2, 0)

        @pl.when(p < panels - 3)
        def _():
            stage_own(p + 3)

        th, tl = split(jnp.where(upper, tin[p], 0.0))
        for h in range(2):
            for i in range(1, 4):
                ex_z(p, h, i).wait_recv()
            mh, ml = split((rz[p, h, 0] + rz[p, h, 1]) + (rz[p, h, 2] + rz[p, h, 3]))
            mine = pl.ds(pl.multiple_of(h * half + xi * own, 8), own)
            ct[p, mine] = dot3(mh, ml, th, tl, NT)
            for i in range(1, 4):
                ag_x(p, h, i).start()

        each(p * 2, p * 2 + 2, lambda i: move_soon(i).start())

        @pl.when(p < panels - 2)
        def _():
            stage_peer(p + 2)

        @pl.when(p < panels - 1)
        def _():
            stage_far(p + 1, 0)
            stage_far(p + 1, 1)
            stage_end(p + 1)

    for h in range(2):
        for i in range(1, 4):
            ag_x(panels - 1, h, i).wait_recv()
    each(0, 8, lambda i: coef(panels - 1, i).start())
    apply(panels - 1, False)

    squares = jnp.zeros((nb, 128), F32)
    for i in range(lanes // 128):
        block = u[:, i * 128 : (i + 1) * 128]
        squares += block * block
    partial = jnp.broadcast_to(jnp.sum(squares.T, axis=0, keepdims=True), (8, nb))
    nsrc[...] = partial
    nrecv[0] = partial
    each(1, 16, lambda i: norms(i).start())
    each(1, 8, lambda i: move_beside(i).start())
    each(1, 16, lambda i: norms(i).wait_recv())
    norm_sq = jnp.sum(nrecv[...], axis=0)
    tall = jnp.broadcast_to(norm_sq[0:1], (128, nb)).T
    scl[...] = lax.rsqrt(tall / total_rows + 1e-06)
    each(1, 16, lambda i: scales(i).start())
    each(0, 8, lambda i: move_across(i).start())

    each(0, 8, lambda i: move_soon(i).wait_recv())

    @pl.loop(0, panels)
    def _(p):
        each(0, 8, lambda i: coef(p, i).wait_recv())
        ch, cl = split(ca[p])

        def body(s):
            ua[:, s] -= dot3(ch, cl, vh[p, :, s], vl[p, :, s], NN)

        chunks(body)

    def store(source):
        return pltpu.make_async_copy(out.at[sixteen(source)], o_ref.at[sixteen(source)], o_s.at[source])

    out[sixteen(col), :] = u[sixteen(col), :] * scl[sixteen(col), 0:1]
    store(col).start()

    def take_beside(i):
        source = col ^ i
        scales(i).wait_recv()
        move_beside(i).wait_recv()
        out[sixteen(source), :] = out[sixteen(source), :] * sclr[sixteen(source), 0:1]
        store(source).start()

    each(1, 8, take_beside)

    def take_across(i):
        source = across(i)
        scales(8 + i).wait_recv()
        low, high = eight(source * 2), eight(source * 2 + 1)
        out[low, :] = ua[eight(ci ^ i), :] * sclr[low, 0:1]
        move_across(i).wait_recv()
        out[high, :] = out[high, :] * sclr[high, 0:1]
        store(source).start()

    each(0, 8, take_across)
    each(0, 16, lambda i: store(i).wait())

    def sent(i):
        norms(i).wait_send()
        scales(i).wait_send()

    each(1, 16, sent)
    each(1, 8, lambda i: move_beside(i).wait_send())

    def sent_across(i):
        move_soon(i).wait_send()
        move_across(i).wait_send()

    each(0, 8, sent_across)

    @pl.loop(0, panels)
    def _(p):
        z_copy(p).wait_send()
        each(0, 8, lambda i: coef(p, i).wait_send())
        for s in range(2):
            for kind in range(4):
                y_copy(p, s, kind).wait_send()
                k_copy(p, s, kind).wait_send()
        for h in range(2):
            for i in range(1, 4):
                rs_x(p, h, i).wait_send()
                ex_z(p, h, i).wait_send()
                ag_x(p, h, i).wait_send()


def local(panel, t_factor, eigvecs):
    panels, lanes, width = panel.shape
    cols = eigvecs.shape[1]
    nb = t_factor.shape[1]
    vt = jnp.transpose(panel, (0, 2, 1))
    total_rows = lanes * lax.axis_size("row")
    vmem, dma = pltpu.VMEM, pltpu.SemaphoreType.DMA
    any_spec = pl.BlockSpec(memory_space=pl.ANY)
    done = pl.pallas_call(
        functools.partial(kernel, total_rows),
        out_shape=jax.ShapeDtypeStruct((cols, lanes), F32),
        in_specs=[any_spec] * 3,
        out_specs=any_spec,
        scratch_shapes=[
            vmem((lanes, cols), F32),
            vmem((panels, nb, nb), F32),
            vmem((panels, nb, lanes), F32),
            vmem((panels, nb, lanes), BF16),
            vmem((panels, nb, lanes), BF16),
            vmem((cols, lanes), F32),
            vmem((cols, lanes), BF16),
            vmem((cols, lanes), BF16),
            vmem((cols, nb), F32),
            vmem((nb, nb), F32),
            vmem((panels, cols, nb), F32),
            vmem((panels, 2, 3, cols // 8, nb), F32),
            vmem((panels, 2, 4, cols // 8, nb), F32),
            vmem((panels, cols, nb), F32),
            vmem((cols // 4, lanes), F32),
            vmem((cols // 4, lanes), F32),
            vmem((panels, cols // 4, nb), F32),
            vmem((cols, lanes), F32),
            vmem((8, cols), F32),
            vmem((16, 8, cols), F32),
            vmem((cols, 128), F32),
            vmem((cols, 128), F32),
            dma((panels + 2,)),
            dma((panels,)),
            dma((panels,)),
            dma((panels, 8)),
            dma((panels, 8)),
            dma((panels, 8)),
            dma((panels, 8)),
            dma((panels, 18)),
            dma((panels, 18)),
            dma((16,)),
            dma((16,)),
            dma((16,)),
            dma((16,)),
            dma((16,)),
            dma((16,)),
            dma((16,)),
            dma((8,)),
            dma((8,)),
            dma((panels, 8)),
            dma((panels, 8)),
        ],
        compiler_params=pltpu.CompilerParams(
            collective_id=0, has_side_effects=True, vmem_limit_bytes=60 * 2**20
        ),
    )(vt, t_factor, eigvecs)
    return jnp.transpose(done)


def solution(mesh):
    in_specs = (P(None, "row", "col"), P(), P("row", "col"))
    return jax.shard_map(local, mesh=mesh, in_specs=in_specs, out_specs=P("row", "col"), check_vma=False)
```

```python
import functools

import jax
import jax.numpy as jnp
from jax import lax
from jax.experimental import pallas as pl
from jax.experimental.pallas import tpu as pltpu
from jax.sharding import PartitionSpec as P

MESH = pl.DeviceIdType.MESH
F32 = jnp.float32
BF16 = jnp.bfloat16
NT = (((1,), (1,)), ((), ()))
NN = (((1,), (0,)), ((), ()))
CHUNK = 1024


def split(x):
    high = x.astype(BF16)
    return high, (x - high.astype(F32)).astype(BF16)


def dot3(ah, al, bh, bl, dims):
    dot = functools.partial(lax.dot_general, dimension_numbers=dims, preferred_element_type=F32)
    return dot(ah, bh) + dot(ah, bl) + dot(al, bh)


def kernel(
    total_rows, v_hbm, t_hbm, z_hbm, o_ref,
    zin, tin, vg, vh, vl, u, uh, ul, acc, gram, pt, rx, rz, ct, early, ua, ca, out, nsrc, nrecv, scl, sclr,
    loc, z_s, z_r, y_s, y_r, k_s, k_r, r_s, r_r, a_s, a_r, n_s, n_r, s_s, s_r, o_s, e_s, e_r, c_s, c_r,
):
    panels, nb, lanes = vg.shape
    half = u.shape[0] // 2
    own = half // 4
    row, col = lax.axis_index("row"), lax.axis_index("col")
    xi, zi = row // 4, row % 4
    hi, yi, ki = col // 8, (col // 2) % 4, col % 2
    ci = col % 8

    def chip(h, y, k):
        return (row, h * 8 + y * 2 + k)

    z_peer = chip(1 - hi, yi, ki)
    k_peer = chip(hi, yi, 1 - ki)
    right, left, far = (yi + 1) % 4, (yi + 3) % 4, (yi + 2) % 4
    y_right, y_left = chip(hi, right, ki), chip(hi, left, ki)

    def at(p, h, y, start=0, size=16):
        return vg.at[p, pl.ds(pl.multiple_of((h * 8 + y * 2 + ki) * 16 + start, 8), size)]

    def remote(src, dst, send, recv, device):
        return pltpu.make_async_remote_copy(
            src_ref=src, dst_ref=dst, send_sem=send, recv_sem=recv, device_id=device, device_id_type=MESH
        )

    def own_copy(p):
        return pltpu.make_async_copy(v_hbm.at[p], at(p, hi, yi), loc.at[p])

    def z_copy(p):
        return remote(v_hbm.at[p], at(p, hi, yi), z_s.at[p], z_r.at[p], z_peer)

    def side(s):
        return hi if s == 0 else 1 - hi

    def y_copy(p, s, kind):
        h = side(s)
        if kind == 0:
            block, device = at(p, h, yi), y_right
        elif kind == 1:
            block, device = at(p, h, yi), y_left
        elif kind == 2:
            block, device = at(p, h, left, 0, 8), y_right
        else:
            block, device = at(p, h, right, 8, 8), y_left
        i = s * 4 + kind
        return remote(block, block, y_s.at[p, i], y_r.at[p, i], device)

    def k_copy(p, s, which):
        block = at(p, side(s), (yi, left, right, far)[which])
        i = s * 4 + which
        return remote(block, block, k_s.at[p, i], k_r.at[p, i], k_peer)

    def row_peer(dx, dz):
        return (((xi + dx) % 4) * 4 + (zi + dz) % 4, col)

    def part(ref, p, h, x):
        return ref.at[p, pl.ds(pl.multiple_of(h * half + x * own, 8), own)]

    def rs_x(p, h, i):
        to = (xi + i) % 4
        j = h * 9 + i - 1
        return remote(part(pt, p, h, to), rx.at[p, h, i - 1], r_s.at[p, j], r_r.at[p, j], row_peer(i, 0))

    def ex_z(p, h, i):
        j = h * 9 + 2 + i
        block = rz.at[p, h, zi]
        return remote(block, block, r_s.at[p, j], r_r.at[p, j], row_peer(0, i))

    def ag_x(p, h, i):
        j = h * 9 + 5 + i
        block = part(ct, p, h, xi)
        return remote(block, block, r_s.at[p, j], r_r.at[p, j], row_peer(i, 0))

    def eight(i):
        return pl.ds(pl.multiple_of(i * 8, 8), 8)

    def sixteen(i):
        return pl.ds(pl.multiple_of(i * 16, 16), 16)

    def across(i):
        return (1 - hi) * 8 + (ci ^ i)

    def move_soon(i):
        return remote(early.at[eight(ci ^ i)], ua.at[eight(ci)], e_s.at[i], e_r.at[i], (row, across(i)))

    def coef(p, i):
        return remote(ct.at[p, eight(across(i) * 2)], ca.at[p, eight(ci)], c_s.at[p, i], c_r.at[p, i], (row, across(i)))

    def move_across(i):
        return remote(u.at[eight(across(i) * 2 + 1)], out.at[eight(col * 2 + 1)], a_s.at[8 + i], a_r.at[8 + i], (row, across(i)))

    def move_beside(i):
        to = col ^ i
        return remote(u.at[sixteen(to)], out.at[sixteen(col)], a_s.at[i], a_r.at[i], (row, to))

    def norms(i):
        return remote(nsrc, nrecv.at[i], n_s.at[i], n_r.at[i], ((row + i) % 16, col))

    def scales(i):
        to = col ^ i
        return remote(
            scl.at[pl.ds(pl.multiple_of(to * 16, 16), 16)],
            sclr.at[pl.ds(pl.multiple_of(col * 16, 16), 16)],
            s_s.at[i], s_r.at[i], (row, to),
        )

    z_load = pltpu.make_async_copy(z_hbm, zin, loc.at[panels])
    t_load = pltpu.make_async_copy(t_hbm, tin, loc.at[panels + 1])
    for p in range(panels):
        own_copy(p).start()
    z_load.start()
    t_load.start()
    barrier = pltpu.get_barrier_semaphore()

    def greet(i, carry):
        pl.semaphore_signal(barrier, inc=1, device_id=((row + i) % 16, col), device_id_type=MESH)
        pl.semaphore_signal(barrier, inc=1, device_id=(row, (col + i) % 16), device_id_type=MESH)
        return carry

    lax.fori_loop(1, 16, greet, 0)
    for p in range(panels):
        own_copy(p).wait()
    pl.semaphore_wait(barrier, 30)

    def stage_own(p):
        y_copy(p, 0, 0).start()
        y_copy(p, 0, 1).start()
        k_copy(p, 0, 0).start()

    def stage_peer(p):
        z_copy(p).wait_recv()
        y_copy(p, 1, 0).start()
        y_copy(p, 1, 1).start()
        k_copy(p, 1, 0).start()

    def stage_relay(p, s):
        y_copy(p, s, 0).wait_recv()
        y_copy(p, s, 2).start()
        k_copy(p, s, 1).start()
        y_copy(p, s, 1).wait_recv()
        y_copy(p, s, 3).start()
        k_copy(p, s, 2).start()

    def stage_far(p, s):
        y_copy(p, s, 2).wait_recv()
        y_copy(p, s, 3).wait_recv()
        k_copy(p, s, 3).start()

    def stage_end(p):
        for s in range(2):
            for which in range(4):
                k_copy(p, s, which).wait_recv()

    def chunks(body):
        @pl.loop(0, lanes // CHUNK)
        def _(i):
            body(pl.ds(pl.multiple_of(i * CHUNK, CHUNK), CHUNK))

    for p in range(panels):
        z_copy(p).start()
    stage_own(0)
    stage_own(1)

    z_load.wait()
    t_load.wait()

    @pl.loop(0, lanes // 512)
    def _(i):
        s = pl.ds(pl.multiple_of(i * 512, 512), 512)
        block = zin[s, :].T
        u[:, s] = block
        high, low = split(block)
        uh[:, s] = high
        ul[:, s] = low
        crossing = zin[s, pl.ds(pl.multiple_of((1 - hi) * 128, 128), 128)].T.reshape(8, 16, 512)
        early[:, s] = crossing[:, 0:8].reshape(64, 512)

    stage_relay(0, 0)
    stage_peer(0)
    stage_relay(1, 0)
    stage_own(2)
    stage_far(0, 0)
    stage_relay(0, 1)
    stage_peer(1)
    stage_far(0, 1)
    stage_end(0)

    def each(first, last, body):
        def step(i, carry):
            body(i)
            return carry

        lax.fori_loop(first, last, step, 0)

    upper = lax.broadcasted_iota(jnp.int32, (nb, nb), 0) <= lax.broadcasted_iota(jnp.int32, (nb, nb), 1)

    def apply(p, keep):
        ch, cl = split(ct[p])

        def body(s):
            new = u[:, s] - dot3(ch, cl, vh[p, :, s], vl[p, :, s], NN)
            u[:, s] = new
            if keep:
                high, low = split(new)
                uh[:, s] = high
                ul[:, s] = low

        chunks(body)

    @pl.loop(0, panels)
    def _(p):
        @pl.loop(0, nb // 16)
        def _(i):
            s = pl.ds(pl.multiple_of(i * 16, 16), 16)
            high, low = split(vg[p, s, :])
            vh[p, s, :] = high
            vl[p, s, :] = low

        acc[...] = dot3(uh[...], ul[...], vh[p], vl[p], NT)

        @pl.when(p > 0)
        def _():
            gram[...] = dot3(vh[p - 1], vl[p - 1], vh[p], vl[p], NT)
            for h in range(2):
                for i in range(1, 4):
                    ag_x(p - 1, h, i).wait_recv()
            ch, cl = split(ct[p - 1])
            gh, gl = split(gram[...])
            acc[...] -= dot3(ch, cl, gh, gl, NN)

        pt[p] = acc[...]
        for h in range(2):
            for i in range(1, 4):
                rs_x(p, h, i).start()

        @pl.when(p < panels - 1)
        def _():
            stage_relay(p + 1, 1)

        @pl.when(p > 0)
        def _():
            each(0, 8, lambda i: coef(p - 1, i).start())
            apply(p - 1, True)

        for h in range(2):
            for i in range(1, 4):
                rs_x(p, h, i).wait_recv()
            mine = pl.ds(pl.multiple_of(h * half + xi * own, 8), own)
            rz[p, h, zi] = pt[p, mine] + (rx[p, h, 0] + rx[p, h, 1] + rx[p, h, 2])
            for i in range(1, 4):
                ex_z(p, h, i).start()

        @pl.when(p < panels - 2)
        def _():
            stage_relay(p + 2, 0)

        @pl.when(p < panels - 3)
        def _():
            stage_own(p + 3)

        th, tl = split(jnp.where(upper, tin[p], 0.0))
        for h in range(2):
            for i in range(1, 4):
                ex_z(p, h, i).wait_recv()
            mh, ml = split((rz[p, h, 0] + rz[p, h, 1]) + (rz[p, h, 2] + rz[p, h, 3]))
            mine = pl.ds(pl.multiple_of(h * half + xi * own, 8), own)
            ct[p, mine] = dot3(mh, ml, th, tl, NT)
            for i in range(1, 4):
                ag_x(p, h, i).start()

        each(p * 2, p * 2 + 2, lambda i: move_soon(i).start())

        @pl.when(p < panels - 2)
        def _():
            stage_peer(p + 2)

        @pl.when(p < panels - 1)
        def _():
            stage_far(p + 1, 0)
            stage_far(p + 1, 1)
            stage_end(p + 1)

    for h in range(2):
        for i in range(1, 4):
            ag_x(panels - 1, h, i).wait_recv()
    each(0, 8, lambda i: coef(panels - 1, i).start())
    apply(panels - 1, False)

    squares = jnp.zeros((nb, 128), F32)
    for i in range(lanes // 128):
        block = u[:, i * 128 : (i + 1) * 128]
        squares += block * block
    partial = jnp.broadcast_to(jnp.sum(squares.T, axis=0, keepdims=True), (8, nb))
    nsrc[...] = partial
    nrecv[0] = partial
    each(1, 16, lambda i: norms(i).start())
    each(1, 8, lambda i: move_beside(i).start())
    each(1, 16, lambda i: norms(i).wait_recv())
    norm_sq = jnp.sum(nrecv[...], axis=0)
    tall = jnp.broadcast_to(norm_sq[0:1], (128, nb)).T
    scl[...] = lax.rsqrt(tall / total_rows + 1e-06)
    each(1, 16, lambda i: scales(i).start())
    each(0, 8, lambda i: move_across(i).start())

    each(0, 8, lambda i: move_soon(i).wait_recv())

    @pl.loop(0, panels)
    def _(p):
        each(0, 8, lambda i: coef(p, i).wait_recv())
        ch, cl = split(ca[p])

        def body(s):
            ua[:, s] -= dot3(ch, cl, vh[p, :, s], vl[p, :, s], NN)

        chunks(body)

    def store(source):
        return pltpu.make_async_copy(out.at[sixteen(source)], o_ref.at[sixteen(source)], o_s.at[source])

    out[sixteen(col), :] = u[sixteen(col), :] * scl[sixteen(col), 0:1]
    store(col).start()

    def take_beside(i):
        source = col ^ i
        scales(i).wait_recv()
        move_beside(i).wait_recv()
        out[sixteen(source), :] = out[sixteen(source), :] * sclr[sixteen(source), 0:1]
        store(source).start()

    each(1, 8, take_beside)

    def take_across(i):
        source = across(i)
        scales(8 + i).wait_recv()
        low, high = eight(source * 2), eight(source * 2 + 1)
        out[low, :] = ua[eight(ci ^ i), :] * sclr[low, 0:1]
        move_across(i).wait_recv()
        out[high, :] = out[high, :] * sclr[high, 0:1]
        store(source).start()

    each(0, 8, take_across)
    each(0, 16, lambda i: store(i).wait())

    def sent(i):
        norms(i).wait_send()
        scales(i).wait_send()

    each(1, 16, sent)
    each(1, 8, lambda i: move_beside(i).wait_send())

    def sent_across(i):
        move_soon(i).wait_send()
        move_across(i).wait_send()

    each(0, 8, sent_across)

    @pl.loop(0, panels)
    def _(p):
        z_copy(p).wait_send()
        each(0, 8, lambda i: coef(p, i).wait_send())
        for s in range(2):
            for kind in range(4):
                y_copy(p, s, kind).wait_send()
                k_copy(p, s, kind).wait_send()
        for h in range(2):
            for i in range(1, 4):
                rs_x(p, h, i).wait_send()
                ex_z(p, h, i).wait_send()
                ag_x(p, h, i).wait_send()


def local(panel, t_factor, eigvecs):
    panels, lanes, width = panel.shape
    cols = eigvecs.shape[1]
    nb = t_factor.shape[1]
    vt = jnp.transpose(panel, (0, 2, 1))
    total_rows = lanes * lax.axis_size("row")
    vmem, dma = pltpu.VMEM, pltpu.SemaphoreType.DMA
    any_spec = pl.BlockSpec(memory_space=pl.ANY)
    done = pl.pallas_call(
        functools.partial(kernel, total_rows),
        out_shape=jax.ShapeDtypeStruct((cols, lanes), F32),
        in_specs=[any_spec] * 3,
        out_specs=any_spec,
        scratch_shapes=[
            vmem((lanes, cols), F32),
            vmem((panels, nb, nb), F32),
            vmem((panels, nb, lanes), F32),
            vmem((panels, nb, lanes), BF16),
            vmem((panels, nb, lanes), BF16),
            vmem((cols, lanes), F32),
            vmem((cols, lanes), BF16),
            vmem((cols, lanes), BF16),
            vmem((cols, nb), F32),
            vmem((nb, nb), F32),
            vmem((panels, cols, nb), F32),
            vmem((panels, 2, 3, cols // 8, nb), F32),
            vmem((panels, 2, 4, cols // 8, nb), F32),
            vmem((panels, cols, nb), F32),
            vmem((cols // 4, lanes), F32),
            vmem((cols // 4, lanes), F32),
            vmem((panels, cols // 4, nb), F32),
            vmem((cols, lanes), F32),
            vmem((8, cols), F32),
            vmem((16, 8, cols), F32),
            vmem((cols, 128), F32),
            vmem((cols, 128), F32),
            dma((panels + 2,)),
            dma((panels,)),
            dma((panels,)),
            dma((panels, 8)),
            dma((panels, 8)),
            dma((panels, 8)),
            dma((panels, 8)),
            dma((panels, 18)),
            dma((panels, 18)),
            dma((16,)),
            dma((16,)),
            dma((16,)),
            dma((16,)),
            dma((16,)),
            dma((16,)),
            dma((16,)),
            dma((8,)),
            dma((8,)),
            dma((panels, 8)),
            dma((panels, 8)),
        ],
        compiler_params=pltpu.CompilerParams(
            collective_id=0, has_side_effects=True, vmem_limit_bytes=60 * 2**20
        ),
    )(vt, t_factor, eigvecs)
    return jnp.transpose(done)


def solution(mesh):
    in_specs = (P(None, "row", "col"), P(), P("row", "col"))
    return jax.shard_map(local, mesh=mesh, in_specs=in_specs, out_specs=P("row", "col"), check_vma=False)
```
